512 devices in a mesh: pipe: 8 (over z), mp: 16 (over y, core), dp: 4 (over x).
Axes of the slice: x: 4, y: 8, z: 8, core: 2. Of those that a mesh axis runs over, the one named last changes fastest.
Arguments:
- hidden: bfloat16 [49152, 8192], P(('pipe', 'dp'), 'mp'), may hold values from -6 to 6
- latent_head_weight: bfloat16 [8192, 512], P('mp', 'dp'), may hold values from -0.0625 to 0.0625
- stretch_holder: int32 [2048, 2], P(('pipe', 'dp')), may hold values from 0 to 15, as said below
- stretch_position: int32 [2048, 2], P(('pipe', 'dp')), may hold values from 0 to 15, as said below
- stretch_frame_count: int32 [2048, 2], P(('pipe', 'dp')), may hold values from 1 to 12
- upsample_weight: bfloat16 [2, 512, 2048], P(None, 'dp'), may hold values from -0.1875 to 0.1875
- upsample_bias: float32 [256], replicated, may hold values from -3 to 3
- snake_alpha_first: float32 [256], replicated, may hold values from 0.5 to 4
- dilated_weight: bfloat16 [3, 256, 256], replicated, may hold values from -0.21875 to 0.21875
- snake_alpha_second: float32 [256], replicated, may hold values from 0.5 to 4
- pointwise_weight: bfloat16 [256, 256], replicated, may hold values from -0.375 to 0.375
Outputs:
- vocoded: bfloat16 [8, 256, 4, 96, 256], P('pipe', 'mp', 'dp')
The draws below stay inside these ranges and needn't reach their ends.
Inputs may be any that keep to these rules, and one draw needn't show every extreme that they name: `stretch_holder`: streams g * 64 to (g + 1) * 64 - 1 form vocoder group g. In each group every owner is named by at most 16 stretches, and one owner by exactly 16. The 8 stretches of each aligned block of 4 streams of a group name one owner at most 2 times, and some block does so exactly 2 times. `stretch_position`: within a group, the stretches of one owner hold the slots 0 up to their number minus one, each once.
All inputs are finite; a program needn't handle non-finite values.
Results may differ from the reference program's by a relative error of at most 0.007.
Values may be sent and summed in bfloat16 or wider, within the bound.
A program may use at most 64 MiB of HBM per device.

```python
import math
import jax
import jax.numpy as jnp
from jax import lax

D = 8192
LATENT = 512
UPSAMPLE_CHANNELS = 256
STRIDE = 8
DILATION_RATE = 3
STRETCH = 12
S_DEV = 4
STREAMS_GROUP = 64
GROUPS = 32
STREAMS = 2048
ROWS = 49152
RECV_CAP = 16
N_PIPE = 8
N_MP = 16
N_DP = 4


def shuffle_one(sub_key):
    return jax.random.permutation(sub_key, 2 * S_DEV).astype(jnp.int32)


def route_group(group_key):
    owners_n = N_MP
    per_source = 2 * S_DEV
    item_total = per_source * owners_n
    keys = jax.random.split(group_key, 5)
    shift_amount = jax.random.randint(keys[0], (owners_n // 2,), 0, per_source).astype(jnp.int32)
    shift_amount = shift_amount.at[0].set(per_source)
    owner_loads = jnp.stack([per_source + shift_amount, per_source - shift_amount], axis=1).reshape(owners_n)
    run_ends = jnp.cumsum(owner_loads)
    positions = jnp.arange(item_total, dtype=jnp.int32)
    run_label = jnp.sum((run_ends[None, :] <= positions[:, None]).astype(jnp.int32), axis=1)
    owner_perm = jax.random.permutation(keys[1], owners_n).astype(jnp.int32)
    pos_owner = owner_perm[run_label]
    source_perm = jax.random.permutation(keys[2], owners_n).astype(jnp.int32)
    pos_source = source_perm[positions // 2 % owners_n]
    within = positions // (2 * owners_n) * 2 + positions % 2
    shuffles = jax.vmap(shuffle_one)(jax.random.split(keys[3], owners_n))
    pos_item = pos_source * per_source + shuffles[pos_source, within]
    ranking = jax.random.permutation(keys[4], item_total).astype(jnp.int32)
    same_owner = pos_owner[:, None] == pos_owner[None, :]
    pos_slot = jnp.sum((same_owner & (ranking[None, :] < ranking[:, None])).astype(jnp.int32), axis=1)
    owner_items = jnp.zeros((item_total,), jnp.int32).at[pos_item].set(pos_owner)
    slot_entries = jnp.zeros((item_total,), jnp.int32).at[pos_item].set(pos_slot)
    return (owner_items, slot_entries)


def routing_tables(base_key):

    def keyed(group_number):
        return route_group(jax.random.fold_in(base_key, group_number))
    owner_all, slot_all = jax.vmap(keyed)(jnp.arange(N_PIPE * N_DP, dtype=jnp.int32))
    return (owner_all.reshape(STREAMS, 2), slot_all.reshape(STREAMS, 2))


def draw_stretch_holder(key, part):
    return routing_tables(key)[0]


def draw_stretch_position(key, part):
    return routing_tables(key)[1]


def touch_ends(drawn, stream_key, least, high):
    index_at = [jax.random.randint(jax.random.fold_in(stream_key, axis), (), 0, length) for axis, length in enumerate(drawn.shape)]
    main_axis = drawn.shape.index(max(drawn.shape))
    beside = index_at[:main_axis] + [(index_at[main_axis] + 1) % drawn.shape[main_axis]] + index_at[main_axis + 1:]
    return drawn.at[tuple(index_at)].set(least).at[tuple(beside)].set(high)


def level_of(key, shape, cuts, smallest, largest):
    factor_of = 1.0
    for axis_at, parts in cuts:
        steps = jax.random.uniform(jax.random.fold_in(jax.random.fold_in(key, 6), axis_at), (parts,), jnp.float32, smallest / len(cuts), largest / len(cuts))
        factor_of = factor_of * jnp.repeat(jnp.exp(steps), shape[axis_at] // parts).reshape((-1,) + (1,) * (len(shape) - 1 - axis_at))
    return factor_of


def scatter_about(key, dims, deviation, bound, pieces=(), kind=jnp.bfloat16):
    drawn = deviation * jax.random.normal(key, dims, jnp.float32)
    if pieces:
        drawn = drawn * level_of(key, dims, pieces, -0.22, 0.18)
    return jnp.clip(drawn, -bound, bound).astype(kind)


def setup_inputs(seed: int = 0) -> dict:
    seeds = jax.random.split(jax.random.key(seed), 12)
    return {
        "hidden": scatter_about(seeds[0], (ROWS, D), 1.0, 6.0, ((0, 32), (1, 16))),
        "latent_head_weight": scatter_about(seeds[1], (D, LATENT), D ** -0.5, 0.0625, ((0, 16), (1, 4))),
        "stretch_holder": draw_stretch_holder(jax.random.fold_in(seeds[11], 71), 0),
        "stretch_position": draw_stretch_position(jax.random.fold_in(seeds[11], 71), 0),
        "stretch_frame_count": touch_ends(jax.random.randint(seeds[4], (STREAMS, 2), 1, STRETCH + 1), jax.random.fold_in(seeds[4], 1), 1, STRETCH).astype(jnp.int32),
        "upsample_weight": scatter_about(seeds[5], (2, LATENT, STRIDE * UPSAMPLE_CHANNELS), (2 * LATENT) ** -0.5, 0.1875, ((1, 4),)),
        "upsample_bias": scatter_about(seeds[6], (UPSAMPLE_CHANNELS,), 0.5, 3.0, (), jnp.float32),
        "snake_alpha_first": jnp.clip(jnp.exp(jax.random.uniform(seeds[7], (UPSAMPLE_CHANNELS,), jnp.float32, math.log(0.5), math.log(4.0))), 0.5, 4.0),
        "dilated_weight": scatter_about(seeds[8], (3, UPSAMPLE_CHANNELS, UPSAMPLE_CHANNELS), (3 * UPSAMPLE_CHANNELS) ** -0.5, 0.21875),
        "snake_alpha_second": jnp.clip(jnp.exp(jax.random.uniform(seeds[9], (UPSAMPLE_CHANNELS,), jnp.float32, math.log(0.5), math.log(4.0))), 0.5, 4.0),
        "pointwise_weight": scatter_about(seeds[10], (UPSAMPLE_CHANNELS, UPSAMPLE_CHANNELS), UPSAMPLE_CHANNELS ** -0.5, 0.375),
    }


def snake_act(signal, alpha_rate):
    return signal + jnp.sin(alpha_rate * signal) ** 2 / alpha_rate


def reference(hidden, latent_head_weight, stretch_holder, stretch_position, stretch_frame_count, upsample_weight, upsample_bias, snake_alpha_first, dilated_weight, snake_alpha_second, pointwise_weight):
    seq_len = 2 * STRETCH
    group_rows = STREAMS_GROUP * seq_len
    samples = seq_len * STRIDE

    def one_group(group_index):
        state_rows = lax.dynamic_slice_in_dim(hidden, group_index * group_rows, group_rows, 0)
        owner_list = lax.dynamic_slice_in_dim(stretch_holder, group_index * STREAMS_GROUP, STREAMS_GROUP, 0)
        slot_list = lax.dynamic_slice_in_dim(stretch_position, group_index * STREAMS_GROUP, STREAMS_GROUP, 0)
        counts = lax.dynamic_slice_in_dim(stretch_frame_count, group_index * STREAMS_GROUP, STREAMS_GROUP, 0)
        latent = jnp.dot(state_rows, latent_head_weight, preferred_element_type=jnp.float32).astype(jnp.bfloat16)
        latent = latent.reshape(STREAMS_GROUP, seq_len, LATENT)
        first_count = counts[:, 0:1]
        second = counts[:, 1:2]
        steps_t = jnp.arange(seq_len, dtype=jnp.int32)[None, :]
        source = jnp.where(steps_t < first_count, steps_t, steps_t - first_count + STRETCH)
        source = jnp.clip(source, 0, seq_len - 1).astype(jnp.int32)
        living = steps_t < first_count + second
        frames = jnp.take_along_axis(latent, source[:, :, None], axis=1)
        frames = jnp.where(living[:, :, None], frames, jnp.zeros((), jnp.bfloat16))
        before = jnp.concatenate([jnp.zeros((STREAMS_GROUP, 1, LATENT), jnp.bfloat16), frames[:, :-1]], axis=1)
        upsampled = jnp.dot(frames.reshape(-1, LATENT), upsample_weight[0], preferred_element_type=jnp.float32)
        upsampled = upsampled + jnp.dot(before.reshape(-1, LATENT), upsample_weight[1], preferred_element_type=jnp.float32)
        upsampled = upsampled.reshape(STREAMS_GROUP, seq_len, STRIDE, UPSAMPLE_CHANNELS) + upsample_bias
        upsampled = upsampled * living.astype(jnp.float32)[:, :, None, None]
        upsampled = upsampled.reshape(STREAMS_GROUP, samples, UPSAMPLE_CHANNELS)
        first_activation = snake_act(upsampled, snake_alpha_first).astype(jnp.bfloat16)
        padded_input = jnp.pad(first_activation, ((0, 0), (2 * DILATION_RATE, 0), (0, 0)))
        dilated_output = jnp.zeros((STREAMS_GROUP * samples, UPSAMPLE_CHANNELS), jnp.float32)
        for kernel_tap_index in range(3):
            frame_offset = 2 * DILATION_RATE - kernel_tap_index * DILATION_RATE
            kernel_tap_input = padded_input[:, frame_offset:frame_offset + samples].reshape(-1, UPSAMPLE_CHANNELS)
            dilated_output = dilated_output + jnp.dot(kernel_tap_input, dilated_weight[kernel_tap_index], preferred_element_type=jnp.float32)
        second_act = snake_act(dilated_output, snake_alpha_second).astype(jnp.bfloat16)
        pointwise = jnp.dot(second_act, pointwise_weight, preferred_element_type=jnp.float32)
        full_out = upsampled + pointwise.reshape(STREAMS_GROUP, samples, UPSAMPLE_CHANNELS)
        full_out = full_out.reshape(STREAMS_GROUP, seq_len, STRIDE * UPSAMPLE_CHANNELS)
        frame_index = jnp.arange(STRETCH, dtype=jnp.int32)[None, :]
        pick_index = jnp.stack([jnp.broadcast_to(frame_index, (STREAMS_GROUP, STRETCH)), first_count + frame_index], axis=1)
        pick_index = pick_index.reshape(STREAMS_GROUP, 2 * STRETCH).astype(jnp.int32)
        kept_mask = frame_index[:, None, :] < counts[:, :, None]
        stretches = jnp.take_along_axis(full_out, pick_index[:, :, None], axis=1)
        stretches = stretches.reshape(STREAMS_GROUP, 2, STRETCH, STRIDE * UPSAMPLE_CHANNELS)
        stretches = jnp.where(kept_mask[:, :, :, None], stretches, 0.0).astype(jnp.bfloat16)
        place_index = (owner_list * RECV_CAP + slot_list).reshape(-1).astype(jnp.int32)
        unit_output = jnp.zeros((N_MP * RECV_CAP, STRETCH, STRIDE * UPSAMPLE_CHANNELS), jnp.bfloat16)
        unit_output = unit_output.at[place_index].set(stretches.reshape(2 * STREAMS_GROUP, STRETCH, STRIDE * UPSAMPLE_CHANNELS))
        return unit_output.reshape(N_MP * RECV_CAP, STRETCH * STRIDE, UPSAMPLE_CHANNELS)

    every_group = lax.map(one_group, jnp.arange(GROUPS, dtype=jnp.int32))
    every_group = every_group.reshape(N_PIPE, N_DP, N_MP * RECV_CAP, STRETCH * STRIDE, UPSAMPLE_CHANNELS)
    return jnp.transpose(every_group, (0, 2, 1, 3, 4))
```

```python
import functools

import jax
import jax.numpy as jnp
from jax import lax
from jax.experimental import pallas as pl
from jax.experimental.pallas import tpu as pltpu
from jax.sharding import PartitionSpec as P

DILATION_RATE = 3
CTX = 2


def item_layout(counts, frames_item, stretch_len):
    stream_total = counts.shape[0]
    context = frames_item - stretch_len
    frame_place = jnp.arange(frames_item, dtype=jnp.int32)[None, :]
    stretch_frame = jnp.broadcast_to(frame_place - context, (stream_total, frames_item))
    first_count = counts[:, 0:1]
    second = counts[:, 1:2]
    alive_first = (stretch_frame >= 0) & (stretch_frame < first_count)
    rows_second = jnp.where(
        stretch_frame < 0, first_count + stretch_frame, stretch_len + stretch_frame
    )
    alive_second = jnp.where(
        stretch_frame < 0, first_count + stretch_frame >= 0, stretch_frame < second
    )
    item_rows = jnp.clip(jnp.stack([stretch_frame, rows_second], axis=1), 0, 2 * stretch_len - 1)
    item_active_mask = jnp.stack([alive_first, alive_second], axis=1)
    return (item_rows, item_active_mask)


SIN2 = (
    9.869604110717773,
    -32.469669342041016,
    42.727195739746094,
    -30.101465225219727,
    13.05009937286377,
    -3.3565926551818848,
)


def snake(v, turns, inverse):
    u = v * turns
    r = u - jnp.round(u)
    s = r * r
    q = jnp.full_like(s, SIN2[-1])
    for c in SIN2[-2::-1]:
        q = q * s + c
    return v + (q * s) * inverse


def vocode(slots, frames, stride, tab, x_ref, wup, bias, a1, dw, a2, pw, out_ref, up, act, out32):
    rows = frames * slots
    live = rows - 2 * slots
    width = bias.shape[1]
    half = width // 2
    span = (frames - 2) * stride
    lane = lax.broadcasted_iota(jnp.int32, (slots, width), 0)
    count = jnp.zeros((slots, width), jnp.int32)
    second = jnp.zeros((slots, width), jnp.int32)
    for s in range(slots):
        word = tab(s)
        count = jnp.where(lane == s, (word // 2) % 16, count)
        second = jnp.where(lane == s, (word // 256) % 2, second)
    turns1 = a1[...] * (1.0 / jnp.pi)
    inv1 = 1.0 / a1[...]
    turns2 = a2[...] * (1.0 / jnp.pi)
    inv2 = 1.0 / a2[...]
    x1 = x_ref[pl.ds(slots, rows - slots), :]
    x0 = x_ref[pl.ds(0, rows - slots), :]

    def first(r, carry):
        col = pl.ds(pl.multiple_of(r * width, width), width)
        u = jnp.dot(x1, wup[0, :, col], preferred_element_type=jnp.float32)
        u = u + jnp.dot(x0, wup[1, :, col], preferred_element_type=jnp.float32) + bias[...]
        u = jnp.concatenate([jnp.where(second > 0, u[:slots], 0.0), u[slots:]], axis=0)
        up[r] = u[slots:]
        act[r] = snake(u, turns1, inv1).astype(jnp.bfloat16)
        return carry

    lax.fori_loop(0, stride, first, 0)

    def tap(r, back):
        s = r - back
        same = s >= 0
        which = jnp.where(same, s, s + stride)
        start = pl.multiple_of(jnp.where(same, slots, 0), slots)
        return act[which, pl.ds(start, live), :]

    def second_half(r, carry):
        d = jnp.dot(tap(r, 0), dw[0], preferred_element_type=jnp.float32)
        d = d + jnp.dot(tap(r, DILATION_RATE), dw[1], preferred_element_type=jnp.float32)
        d = d + jnp.dot(tap(r, 2 * DILATION_RATE), dw[2], preferred_element_type=jnp.float32)
        b = snake(d, turns2, inv2).astype(jnp.bfloat16)
        o = up[r] + jnp.dot(b, pw[...], preferred_element_type=jnp.float32)
        for t in range(frames - 2):
            piece = jnp.where(count > t, o[t * slots : (t + 1) * slots], 0.0)
            at = pl.ds(t * stride + r, slots, stride=span)
            out32[0, at, :] = piece[:, :half]
            out32[1, at, :] = piece[:, half:]
        return carry

    lax.fori_loop(0, stride, second_half, 0)

    def pack(s, carry):
        at = pl.ds(pl.multiple_of(s * span, span), span)
        out_ref[s] = jnp.concatenate([out32[0, at, :], out32[1, at, :]], axis=1).astype(
            out_ref.dtype
        )
        return carry

    lax.fori_loop(0, slots, pack, 0)


def vocoder_kernel(slots, frames, stride, tab, x, wup, bias, a1, dw, a2, pw, out, up, act, out32):
    vocode(
        slots, frames, stride, lambda s: tab[s],
        x, wup, bias, a1, dw, a2, pw, out, up, act, out32,
    )


def vocoder(tab, x, wup, bias, a1, dw, a2, pw, slots, frames, stride):
    rows, width = x.shape[0], bias.shape[0]
    span = (frames - 2) * stride
    vmem = pl.BlockSpec(memory_space=pltpu.VMEM)
    return pl.pallas_call(
        functools.partial(vocoder_kernel, slots, frames, stride),
        out_shape=jax.ShapeDtypeStruct((slots, span, width), jnp.bfloat16),
        in_specs=[pl.BlockSpec(memory_space=pltpu.SMEM)] + [vmem] * 7,
        out_specs=vmem,
        scratch_shapes=[
            pltpu.VMEM((stride, rows - 2 * slots, width), jnp.float32),
            pltpu.VMEM((stride, rows - slots, width), jnp.bfloat16),
            pltpu.VMEM((2, slots * span, width // 2), jnp.float32),
        ],
        compiler_params=pltpu.CompilerParams(vmem_limit_bytes=48 * 2**20),
    )(tab, x, wup, bias[None], a1[None], dw, a2[None], pw)


def body(
    hidden,
    latent_head_weight,
    stretch_holder,
    stretch_position,
    stretch_frame_count,
    upsample_weight,
    upsample_bias,
    snake_alpha_first,
    dilated_weight,
    snake_alpha_second,
    pointwise_weight,
):
    peer_count = lax.axis_size("mp")
    self_index = lax.axis_index("mp")
    head_weight = lax.all_gather(latent_head_weight, "dp", axis=1, tiled=True)
    own_rows = hidden.shape[0] // peer_count
    latent = lax.psum_scatter(
        jnp.dot(hidden, head_weight, preferred_element_type=jnp.float32),
        "mp",
        scatter_dimension=0,
        tiled=True,
    ).astype(jnp.bfloat16)
    group_streams = stretch_frame_count.shape[0]
    per_device = group_streams // peer_count
    seq_len = own_rows // per_device
    stretch_len = seq_len // 2
    frames_item = stretch_len + CTX
    latent_width = latent.shape[1]
    up_width = upsample_bias.shape[0]
    samples = stretch_len * (upsample_weight.shape[2] // up_width)
    item_rows, item_active_mask = item_layout(stretch_frame_count, frames_item, stretch_len)
    my_rows = lax.dynamic_slice_in_dim(item_rows, self_index * per_device, per_device, 0)
    my_rows = my_rows.reshape(per_device, 2 * frames_item)
    my_alive = lax.dynamic_slice_in_dim(item_active_mask, self_index * per_device, per_device, 0)
    my_alive = my_alive.reshape(2 * per_device, frames_item)
    stream_latent = latent.reshape(per_device, seq_len, latent_width)
    picked = jnp.take_along_axis(stream_latent, my_rows[:, :, None], axis=1)
    picked = picked.reshape(2 * per_device, frames_item, latent_width)
    my_items = jnp.where(my_alive[:, :, None], picked, jnp.zeros((), jnp.bfloat16))
    owner_list = stretch_holder.reshape(-1)
    slot_list = stretch_position.reshape(-1)
    item_total = owner_list.shape[0]
    items_device = 2 * per_device
    recv_cap = 2 * items_device
    send_cap = 2 * ((items_device + peer_count - 1) // peer_count)
    item_order = jnp.arange(item_total, dtype=jnp.int32)
    source = item_order // items_device
    earlier = (source[:, None] == source[None, :]) & (owner_list[:, None] == owner_list[None, :])
    earlier = earlier & (item_order[None, :] < item_order[:, None])
    send_slot = jnp.sum(earlier.astype(jnp.int32), axis=1)
    position = source * send_cap + send_slot
    target = owner_list * send_cap + send_slot
    matched = (
        (owner_list[None, :] == self_index)
        & (slot_list[None, :] == jnp.arange(recv_cap, dtype=jnp.int32)[:, None])
    ).astype(jnp.int32)
    chosen_item = jnp.sum(matched * item_order[None, :], axis=1)
    present = jnp.sum(matched, axis=1) > 0
    fetch_index = jnp.sum(matched * position[None, :], axis=1)
    my_target = lax.dynamic_slice_in_dim(target, self_index * items_device, items_device, 0)
    outgoing = (
        jnp.zeros((peer_count * send_cap, frames_item, latent_width), jnp.bfloat16)
        .at[my_target]
        .set(my_items)
    )
    outgoing = outgoing.reshape(peer_count, send_cap * frames_item, latent_width)
    arrived = lax.all_to_all(outgoing, "mp", split_axis=0, concat_axis=0, tiled=True)
    arrived = arrived.reshape(peer_count * send_cap, frames_item, latent_width)
    slot_entries = arrived[fetch_index]
    chosen_count = stretch_frame_count.reshape(-1)[chosen_item]
    tab = jnp.where(present, 1 + chosen_count * 2 + chosen_item * 256, 0).astype(jnp.int32)
    stride_len = upsample_weight.shape[2] // up_width
    wup = lax.all_gather(upsample_weight, "dp", axis=1, tiled=True)
    x = jnp.transpose(slot_entries, (1, 0, 2)).reshape(frames_item * recv_cap, latent_width)
    unit_output = vocoder(
        tab, x, wup, upsample_bias, snake_alpha_first, dilated_weight,
        snake_alpha_second, pointwise_weight, recv_cap, frames_item, stride_len,
    )
    return unit_output.reshape(1, recv_cap, 1, samples, up_width)


def solution(mesh):
    in_specs = (
        P(("pipe", "dp"), "mp"),
        P("mp", "dp"),
        P(("pipe", "dp"), None),
        P(("pipe", "dp"), None),
        P(("pipe", "dp"), None),
        P(None, "dp", None),
        P(),
        P(),
        P(),
        P(),
        P(),
    )
    out_specs = P("pipe", "mp", "dp", None, None)
    return jax.shard_map(body, mesh=mesh, in_specs=in_specs, out_specs=out_specs, check_vma=False)
```

```python
import functools

import jax
import jax.numpy as jnp
from jax import lax
from jax.experimental import pallas as pl
from jax.experimental.pallas import tpu as pltpu
from jax.sharding import PartitionSpec as P

DILATION_RATE = 3
CTX = 2
TILE = 16
BLOCKS = 4
MESH = pl.DeviceIdType.MESH

SIN2 = (
    9.869604110717773,
    -32.469669342041016,
    42.727195739746094,
    -30.101465225219727,
    13.05009937286377,
    -3.3565926551818848,
)


def snake(v, turns, inverse):
    u = v * turns
    r = u - jnp.round(u)
    s = r * r
    q = jnp.full_like(s, SIN2[-1])
    for c in SIN2[-2::-1]:
        q = q * s + c
    return v + (q * s) * inverse


def vocode(slots, frames, stride, tab, x_ref, wup, bias, a1, dw, a2, pw, out_ref, up, act, out32):
    rows = frames * slots
    live = rows - CTX * slots
    width = bias.shape[1]
    half = width // 2
    span = (frames - CTX) * stride
    lane = lax.broadcasted_iota(jnp.int32, (slots, width), 0)
    count = jnp.zeros((slots, width), jnp.int32)
    second = jnp.zeros((slots, width), jnp.int32)
    for s in range(slots):
        word = tab(s)
        count = jnp.where(lane == s, (word // 2) % 16, count)
        second = jnp.where(lane == s, (word // 256) % 2, second)
    turns1 = a1[...] * (1.0 / jnp.pi)
    inv1 = 1.0 / a1[...]
    turns2 = a2[...] * (1.0 / jnp.pi)
    inv2 = 1.0 / a2[...]
    x1 = x_ref[pl.ds(slots, rows - slots), :]
    x0 = x_ref[pl.ds(0, rows - slots), :]

    def first(r, carry):
        col = pl.ds(pl.multiple_of(r * width, width), width)
        u = jnp.dot(x1, wup[0, :, col], preferred_element_type=jnp.float32)
        u = u + jnp.dot(x0, wup[1, :, col], preferred_element_type=jnp.float32) + bias[...]
        u = jnp.concatenate([jnp.where(second > 0, u[:slots], 0.0), u[slots:]], axis=0)
        up[r] = u[slots:]
        act[r] = snake(u, turns1, inv1).astype(jnp.bfloat16)
        return carry

    lax.fori_loop(0, stride, first, 0)

    def tap(r, back):
        s = r - back
        same = s >= 0
        which = jnp.where(same, s, s + stride)
        start = pl.multiple_of(jnp.where(same, slots, 0), slots)
        return act[which, pl.ds(start, live), :]

    def second_half(r, carry):
        d = jnp.dot(tap(r, 0), dw[0], preferred_element_type=jnp.float32)
        d = d + jnp.dot(tap(r, DILATION_RATE), dw[1], preferred_element_type=jnp.float32)
        d = d + jnp.dot(tap(r, 2 * DILATION_RATE), dw[2], preferred_element_type=jnp.float32)
        b = snake(d, turns2, inv2).astype(jnp.bfloat16)
        o = up[r] + jnp.dot(b, pw[...], preferred_element_type=jnp.float32)
        for t in range(frames - CTX):
            piece = jnp.where(count > t, o[t * slots : (t + 1) * slots], 0.0)
            at = pl.ds(t * stride + r, slots, stride=span)
            out32[0, at, :] = piece[:, :half]
            out32[1, at, :] = piece[:, half:]
        return carry

    lax.fori_loop(0, stride, second_half, 0)

    def pack(s, carry):
        at = pl.ds(pl.multiple_of(s * span, span), span)
        out_ref[s] = jnp.concatenate([out32[0, at, :], out32[1, at, :]], axis=1).astype(
            out_ref.dtype
        )
        return carry

    lax.fori_loop(0, slots, pack, 0)


def kernel(
    slots, frames, stride, n_z, n_y, n_x,
    tab, src, hidden, head, wupin, bias, a1, dw, a2, pw,
    out,
    hid, hpad, tiles, hperm, hw, pbuf, sib, rx0, rx, tx0, tx, x, wup, up, act, out32,
    local_sem, head_s, head_r, pair_s, pair_r, ring_s, ring_r, upx_s, upx_r, upz_s, upz_r, upc_s, upc_r,
):
    zi, mi, xi = lax.axis_index("pipe"), lax.axis_index("mp"), lax.axis_index("dp")
    y, c = lax.div(mi, 2), lax.rem(mi, 2)
    rows = frames * slots
    mid = rows // 2
    cols = head.shape[1]

    def peer(dz=0, dy=0, dc=0, dx=0):
        return (
            lax.rem(zi + dz + n_z, n_z),
            lax.rem(y + dy + n_y, n_y) * 2 + lax.rem(c + dc, 2),
            lax.rem(xi + dx + n_x, n_x),
        )

    sibling = peer(dc=1)
    ring = (peer(dy=1), peer(dy=-1))
    across = (peer(dx=1), peer(dx=-1), peer(dx=2))
    origin = (lax.rem(xi + n_x - 1, n_x), lax.rem(xi + 1, n_x), lax.rem(xi + 2, n_x))
    updown = (peer(dz=1), peer(dz=-1))
    sent = []

    def remote(src_ref, dst_ref, s, r, to):
        return pltpu.make_async_remote_copy(
            src_ref=src_ref, dst_ref=dst_ref, send_sem=s, recv_sem=r, device_id=to, device_id_type=MESH
        )

    def send(*a):
        copy = remote(*a)
        copy.start()
        sent.append(copy)

    def arrived(ref, s, r):
        remote(ref, ref, s, r, sibling).wait_recv()

    load = pltpu.make_async_copy(hidden, hid, local_sem.at[0])
    load.start()
    piece = wupin.shape[1]
    own_up = pltpu.make_async_copy(
        wupin, wup.at[:, pl.ds(pl.multiple_of(xi * piece, piece), piece), :], local_sem.at[1]
    )
    own_up.start()
    barrier = pltpu.get_barrier_semaphore()
    for other in (sibling, *ring, *across, *updown):
        pl.semaphore_signal(barrier, inc=1, device_id=other, device_id_type=MESH)
    load.wait()

    n_groups, per = src.shape
    rows_in = hid.shape[0] // n_groups
    tiles_in = per // TILE

    def pad(g, carry):
        row = lax.broadcasted_iota(jnp.int32, (rows_in, per), 0)
        pick = jnp.where(row == src[pl.ds(g, 1), :], 1.0, 0.0).astype(jnp.bfloat16)
        h = hid[pl.ds(pl.multiple_of(g * rows_in, rows_in), rows_in), :]
        got = lax.dot_general(
            pick, h, (((0,), (0,)), ((), ())), preferred_element_type=jnp.float32
        ).astype(jnp.bfloat16)
        hpad[pl.ds(g * tiles_in, tiles_in)] = got.reshape(tiles_in, TILE, got.shape[1])
        return carry

    lax.fori_loop(0, n_groups, pad, 0)

    i = lax.broadcasted_iota(jnp.int32, (rows, slots * TILE), 0)
    j = lax.broadcasted_iota(jnp.int32, (rows, slots * TILE), 1)
    turn = jnp.where((i % slots) * TILE + i // slots == j, 1.0, 0.0).astype(jnp.bfloat16)

    def gather(n, carry):
        part, k = lax.div(n, n_y), lax.rem(n, n_y)
        owner = lax.rem(y + k, n_y) * 2 + lax.rem(c + 1 + part, 2)
        for s in range(slots):
            item = tab[owner * slots + s] // 256
            tiles[s * TILE : (s + 1) * TILE, :] = hpad[item]
        hperm[part, k] = jnp.dot(turn, tiles[...], preferred_element_type=jnp.float32).astype(
            jnp.bfloat16
        )
        return carry

    lax.fori_loop(0, 2 * n_y, gather, 0)

    def project(b, part):
        def one(k, carry):
            w = head[...] if b == 0 else hw[b - 1]
            pbuf[b, part, k] = jnp.dot(
                hperm[part, k], w, preferred_element_type=jnp.float32
            ).astype(jnp.bfloat16)
            return carry

        lax.fori_loop(0, n_y, one, 0)

    project(0, 0)
    project(0, 1)
    pl.semaphore_wait(barrier, 8)

    def pair(b):
        send(pbuf.at[b, 0], sib.at[b], pair_s.at[b], pair_r.at[b], sibling)

    def own(b, k):
        return pbuf[b, 1, k].astype(jnp.float32) + sib[b, k].astype(jnp.float32)

    def step(b, s):
        if s == 0:
            arrived(sib.at[b], pair_s.at[b], pair_r.at[b])
            v = own(b, n_y // 2).astype(jnp.bfloat16)
            tx0[b, 0] = v[:mid]
            tx0[b, 1] = v[mid:]
            for d in range(2):
                send(tx0.at[b, d], rx0.at[b, d], ring_s.at[b, d, 0], ring_r.at[b, d, 0], ring[d])
            return
        for d in range(2):
            k = n_y // 2 - s if d == 0 else n_y // 2 + s
            v = own(b, k)
            if s == 1:
                arrived(rx0.at[b, d], ring_s.at[b, d, 0], ring_r.at[b, d, 0])
                more = rx0[b, d].astype(jnp.float32)
                if d == 0:
                    v = jnp.concatenate([v[:mid] + more, v[mid:]], axis=0)
                else:
                    v = jnp.concatenate([v[:mid], v[mid:] + more], axis=0)
            else:
                arrived(rx.at[b, d, s - 2], ring_s.at[b, d, s - 1], ring_r.at[b, d, s - 1])
                v = v + rx[b, d, s - 2].astype(jnp.float32)
            tx[b, d, s - 1] = v.astype(jnp.bfloat16)
            send(tx.at[b, d, s - 1], rx.at[b, d, s - 1], ring_s.at[b, d, s], ring_r.at[b, d, s], ring[d])

    def final(b):
        v = own(b, 0)
        last = n_y // 2 - 1
        for d in range(2):
            arrived(rx.at[b, d, last - 1], ring_s.at[b, d, last], ring_r.at[b, d, last])
            v = v + rx[b, d, last - 1].astype(jnp.float32)
        q = xi if b == 0 else origin[b - 1]
        x[:, pl.ds(pl.multiple_of(q * cols, cols), cols)] = v.astype(jnp.bfloat16)

    def head_in(j):
        arrived(hw.at[j], head_s.at[j], head_r.at[j])
        project(j + 1, 0)
        pair(j + 1)
        project(j + 1, 1)

    half, quarter = piece // 2, piece // 4
    e = lax.rem(zi, 2)

    def up_rows(q, offset, n):
        return wup.at[:, pl.ds(pl.multiple_of(q * piece + offset, n), n), :]

    def upx_send():
        mine = wupin.at[:, pl.ds(pl.multiple_of(c * half + e * quarter, quarter), quarter), :]
        for j in range(3):
            send(mine, up_rows(xi, c * half + e * quarter, quarter), upx_s.at[j], upx_r.at[j], across[j])

    def upx_in(j):
        at = c * half + e * quarter
        arrived(up_rows(origin[j], at, quarter), upx_s.at[j], upx_r.at[j])
        for d in range(2):
            ref = up_rows(origin[j], at + d * (quarter // 2), quarter // 2)
            send(ref, ref, upz_s.at[j, d], upz_r.at[j, d], updown[d])

    def upz_in(j):
        at = c * half + (1 - e) * quarter
        for d in range(2):
            ref = up_rows(origin[j], at + d * (quarter // 2), quarter // 2)
            arrived(ref, upz_s.at[j, d], upz_r.at[j, d])
        ref = up_rows(origin[j], c * half, half)
        send(ref, ref, upc_s.at[j], upc_r.at[j], sibling)

    def upc_in(j):
        arrived(up_rows(origin[j], (1 - c) * half, half), upc_s.at[j], upc_r.at[j])

    for j in range(3):
        send(head, hw.at[j], head_s.at[j], head_r.at[j], across[j])
    pair(0)
    step(0, 0)
    head_in(0)
    head_in(1)
    upx_send()
    step(0, 1)
    step(1, 0)
    head_in(2)
    step(2, 0)
    step(0, 2)
    step(1, 1)
    step(3, 0)
    step(2, 1)
    step(0, 3)
    step(1, 2)
    step(3, 1)
    step(2, 2)
    final(0)
    upx_in(0)
    step(1, 3)
    step(3, 2)
    step(2, 3)
    upx_in(1)
    final(1)
    step(3, 3)
    upx_in(2)
    upz_in(0)
    upz_in(1)
    final(2)
    upz_in(2)
    final(3)
    for j in range(3):
        upc_in(j)
    own_up.wait()
    for copy in sent:
        copy.wait_send()
    vocode(
        slots, frames, stride, lambda s: tab[mi * slots + s],
        x, wup, bias, a1, dw, a2, pw, out, up, act, out32,
    )


def body(
    hidden,
    latent_head_weight,
    stretch_holder,
    stretch_position,
    stretch_frame_count,
    upsample_weight,
    upsample_bias,
    snake_alpha_first,
    dilated_weight,
    snake_alpha_second,
    pointwise_weight,
):
    n_z, n_mp, n_x = lax.axis_size("pipe"), lax.axis_size("mp"), lax.axis_size("dp")
    n_y = n_mp // 2
    streams = stretch_frame_count.shape[0]
    items = 2 * streams
    seq_len = hidden.shape[0] // streams
    stretch_len = seq_len // 2
    slots = 2 * items // n_mp
    frames = stretch_len + CTX
    rows = frames * slots
    width = upsample_bias.shape[0]
    stride = upsample_weight.shape[2] // width
    span = stretch_len * stride
    depth, cols = latent_head_weight.shape
    latent = cols * n_x

    item = jnp.arange(items, dtype=jnp.int32).reshape(streams, 2)
    key = stretch_holder * slots + stretch_position
    word = 1 + 2 * stretch_frame_count + 256 * item
    place = jnp.arange(n_mp * slots, dtype=jnp.int32)
    tab = jnp.sum(jnp.where(key[:, :, None] == place, word[:, :, None], 0), axis=(0, 1))
    group = TILE // 2
    j = jnp.arange(TILE, dtype=jnp.int32)[None, None, :]
    st = (item % TILE)[:, :, None]
    back = stretch_frame_count[:, 0:1, None] - CTX + j
    back = jnp.where((item[:, :, None] % 2 == 1) & (back >= 0), (st // 2) * seq_len + back, -1)
    here = jnp.where(j < frames, st * stretch_len + j - CTX, -1)
    src = jnp.where(j < CTX, back, here).reshape(streams // group, 2 * group * TILE)

    vmem = pl.BlockSpec(memory_space=pltpu.VMEM)
    anywhere = pl.BlockSpec(memory_space=pl.ANY)
    bf16, f32 = jnp.bfloat16, jnp.float32
    dma = pltpu.SemaphoreType.DMA
    out = pl.pallas_call(
        functools.partial(kernel, slots, frames, stride, n_z, n_y, n_x),
        out_shape=jax.ShapeDtypeStruct((slots, span, width), bf16),
        in_specs=[pl.BlockSpec(memory_space=pltpu.SMEM), vmem, anywhere, vmem, anywhere] + [vmem] * 5,
        out_specs=vmem,
        scratch_shapes=[
            pltpu.VMEM(hidden.shape, bf16),
            pltpu.VMEM((items, TILE, depth), bf16),
            pltpu.VMEM((slots * TILE, depth), bf16),
            pltpu.VMEM((2, n_y, rows, depth), bf16),
            pltpu.VMEM((3, depth, cols), bf16),
            pltpu.VMEM((BLOCKS, 2, n_y, rows, cols), bf16),
            pltpu.VMEM((BLOCKS, n_y, rows, cols), bf16),
            pltpu.VMEM((BLOCKS, 2, rows // 2, cols), bf16),
            pltpu.VMEM((BLOCKS, 2, 3, rows, cols), bf16),
            pltpu.VMEM((BLOCKS, 2, rows // 2, cols), bf16),
            pltpu.VMEM((BLOCKS, 2, 3, rows, cols), bf16),
            pltpu.VMEM((rows, latent), bf16),
            pltpu.VMEM((2, latent, stride * width), bf16),
            pltpu.VMEM((stride, rows - CTX * slots, width), f32),
            pltpu.VMEM((stride, rows - slots, width), bf16),
            pltpu.VMEM((2, slots * span, width // 2), f32),
            dma((2,)),
            dma((3,)), dma((3,)),
            dma((BLOCKS,)), dma((BLOCKS,)),
            dma((BLOCKS, 2, 4)), dma((BLOCKS, 2, 4)),
            dma((3,)), dma((3,)),
            dma((3, 2)), dma((3, 2)),
            dma((3,)), dma((3,)),
        ],
        compiler_params=pltpu.CompilerParams(
            collective_id=0, has_side_effects=True, vmem_limit_bytes=56 * 2**20
        ),
    )(
        tab, src, hidden, latent_head_weight, upsample_weight,
        upsample_bias[None], snake_alpha_first[None], dilated_weight,
        snake_alpha_second[None], pointwise_weight,
    )
    return out.reshape(1, slots, 1, span, width)


def solution(mesh):
    in_specs = (
        P(("pipe", "dp"), "mp"),
        P("mp", "dp"),
        P(("pipe", "dp"), None),
        P(("pipe", "dp"), None),
        P(("pipe", "dp"), None),
        P(None, "dp", None),
        P(),
        P(),
        P(),
        P(),
        P(),
    )
    out_specs = P("pipe", "mp", "dp", None, None)
    return jax.shard_map(body, mesh=mesh, in_specs=in_specs, out_specs=out_specs, check_vma=False)
```

```python
import functools

import jax
import jax.numpy as jnp
from jax import lax
from jax.experimental import pallas as pl
from jax.experimental.pallas import tpu as pltpu
from jax.sharding import PartitionSpec as P

DILATION_RATE = 3
CTX = 2
TILE = 16
BLOCKS = 4
LOADS = 4
MESH = pl.DeviceIdType.MESH

SIN2 = (
    9.869604110717773,
    -32.469669342041016,
    42.727195739746094,
    -30.101465225219727,
    13.05009937286377,
    -3.3565926551818848,
)


def snake(v, turns, inverse):
    u = v * turns
    r = u - jnp.round(u)
    s = r * r
    q = jnp.full_like(s, SIN2[-1])
    for c in SIN2[-2::-1]:
        q = q * s + c
    return v + (q * s) * inverse


def twice(n, step, per=2):
    def some(i, carry):
        for j in range(per):
            step(per * i + j, carry)
        return carry

    lax.fori_loop(0, n // per, some, 0)


def vocode(slots, frames, stride, count, second, x_ref, wup, bias, a1, dw, a2, pw, out_ref, up, act, out32):
    rows = frames * slots
    live = rows - CTX * slots
    width = bias.shape[1]
    half = width // 2
    span = (frames - CTX) * stride
    turns1 = a1[...] * (1.0 / jnp.pi)
    inv1 = 1.0 / a1[...]
    turns2 = a2[...] * (1.0 / jnp.pi)
    inv2 = 1.0 / a2[...]
    x1 = x_ref[pl.ds(slots, rows - slots), :]
    x0 = x_ref[pl.ds(0, rows - slots), :]

    def first(r, carry):
        col = pl.ds(pl.multiple_of(r * width, width), width)
        u = jnp.dot(x1, wup[0, :, col], preferred_element_type=jnp.float32)
        u = u + jnp.dot(x0, wup[1, :, col], preferred_element_type=jnp.float32) + bias[...]
        u = jnp.concatenate([jnp.where(second, u[:slots], 0.0), u[slots:]], axis=0)
        up[r] = u[slots:]
        act[r] = snake(u, turns1, inv1).astype(jnp.bfloat16)
        return carry

    twice(stride, first)

    def tap(r, back):
        s = r - back
        same = s >= 0
        which = jnp.where(same, s, s + stride)
        start = pl.multiple_of(jnp.where(same, slots, 0), slots)
        return act[which, pl.ds(start, live), :]

    def second_half(r, carry):
        d = jnp.dot(tap(r, 0), dw[0], preferred_element_type=jnp.float32)
        d = d + jnp.dot(tap(r, DILATION_RATE), dw[1], preferred_element_type=jnp.float32)
        d = d + jnp.dot(tap(r, 2 * DILATION_RATE), dw[2], preferred_element_type=jnp.float32)
        b = snake(d, turns2, inv2).astype(jnp.bfloat16)
        o = up[r] + jnp.dot(b, pw[...], preferred_element_type=jnp.float32)
        for t in range(frames - CTX):
            piece = jnp.where(count > t, o[t * slots : (t + 1) * slots], 0.0)
            at = pl.ds(t * stride + r, slots, stride=span)
            out32[0, at, :] = piece[:, :half]
            out32[1, at, :] = piece[:, half:]
        return carry

    twice(stride, second_half)

    def pack(s, carry):
        at = pl.ds(pl.multiple_of(s * span, span), span)
        out_ref[s] = jnp.concatenate([out32[0, at, :], out32[1, at, :]], axis=1).astype(
            out_ref.dtype
        )
        return carry

    lax.fori_loop(0, slots, pack, 0)


def kernel(
    slots, frames, stride, n_z, n_y, n_x,
    holder, position, counts, bias, a1, a2, hidden, headin, wupin, dwin, pwin,
    out,
    hid, head, dw, pw, sel, pick, framed, hw2, hw1, pbuf, sib, rx0, rx, tx0, tx, x, wup, up, act, out32,
    local_sem, head_s, head_r, pair_s, pair_r, ring_s, ring_r, upx_s, upx_r, upz_s, upz_r, upc_s, upc_r,
):
    zi, mi, xi = lax.axis_index("pipe"), lax.axis_index("mp"), lax.axis_index("dp")
    y, c = lax.div(mi, 2), lax.rem(mi, 2)
    rows = frames * slots
    mid = rows // 2
    cols = headin.shape[1]

    def peer(dz=0, dy=0, dc=0, dx=0):
        return (
            lax.rem(zi + dz + n_z, n_z),
            lax.rem(y + dy + n_y, n_y) * 2 + lax.rem(c + dc, 2),
            lax.rem(xi + dx + n_x, n_x),
        )

    sibling = peer(dc=1)
    ring = (peer(dy=1), peer(dy=-1))
    across = (peer(dx=1), peer(dx=-1), peer(dx=2))
    origin = (lax.rem(xi + n_x - 1, n_x), lax.rem(xi + 1, n_x), lax.rem(xi + 2, n_x))
    updown = (peer(dz=1), peer(dz=-1))
    sent = []

    def remote(src_ref, dst_ref, s, r, to):
        return pltpu.make_async_remote_copy(
            src_ref=src_ref, dst_ref=dst_ref, send_sem=s, recv_sem=r, device_id=to, device_id_type=MESH
        )

    def send(*a):
        copy = remote(*a)
        copy.start()
        sent.append(copy)

    def arrived(ref, s, r):
        remote(ref, ref, s, r, sibling).wait_recv()

    streams = holder.shape[1]
    items = 2 * streams
    per = TILE // 2
    groups = streams // per
    seq = hid.shape[0] // streams
    half_seq = seq // 2
    rows_in = per * seq
    chunk = hid.shape[0] // LOADS
    loads = [
        pltpu.make_async_copy(
            hidden.at[pl.ds(n * chunk, chunk)], hid.at[pl.ds(n * chunk, chunk)], local_sem.at[n]
        )
        for n in range(LOADS)
    ]
    piece = wupin.shape[1]
    head_load = pltpu.make_async_copy(headin, head, local_sem.at[LOADS])
    others = [
        pltpu.make_async_copy(
            wupin,
            wup.at[:, pl.ds(pl.multiple_of(xi * piece, piece), piece), :],
            local_sem.at[LOADS + 1],
        ),
        pltpu.make_async_copy(dwin, dw, local_sem.at[LOADS + 2]),
        pltpu.make_async_copy(pwin, pw, local_sem.at[LOADS + 3]),
    ]
    for copy in (head_load, *loads, *others):
        copy.start()
    barrier = pltpu.get_barrier_semaphore()
    for other in (sibling, *ring, *across, *updown):
        pl.semaphore_signal(barrier, inc=1, device_id=other, device_id_type=MESH)

    s_of = lax.broadcasted_iota(jnp.int32, (streams, items), 0)
    lane = lax.broadcasted_iota(jnp.int32, (streams, items), 1)
    mine = s_of == lane // TILE * per + lane % per
    late = lane // per % 2 == 1

    eye = lax.broadcasted_iota(jnp.int32, (streams, streams), 0) == lax.broadcasted_iota(
        jnp.int32, (streams, streams), 1
    )

    def column(v):
        return jnp.sum(jnp.where(eye, v, 0), axis=1, keepdims=True)

    def along(first, later):
        v = jnp.where(mine, jnp.where(late, later, first), 0)
        return jnp.sum(v, axis=0, keepdims=True)

    key = holder[...] * slots + position[...]
    length = counts[...]
    c0 = column(length[0:1])
    keys = along(column(key[0:1]), column(key[1:2]))
    lengths = along(c0, column(length[1:2]))

    r = lax.broadcasted_iota(jnp.int32, (n_y * 2 * slots, items), 0)
    core = (r // (n_y * slots) + c + 1) % 2
    owner = (r // slots % n_y + y) % n_y * 2 + core
    pick[...] = jnp.where(keys == owner * slots + r % slots, 1.0, 0.0).astype(jnp.bfloat16)

    own_slot = lax.broadcasted_iota(jnp.int32, (slots, items), 0) + mi * slots
    hit = keys == own_slot
    count = jnp.sum(jnp.where(hit, lengths, 0), axis=1, keepdims=True)
    is_late = lax.broadcasted_iota(jnp.int32, (slots, items), 1) // per % 2
    second = jnp.sum(jnp.where(hit, is_late, 0), axis=1, keepdims=True) > 0

    ri = lax.broadcasted_iota(jnp.int32, (rows - CTX * TILE, rows_in), 0)
    ci = lax.broadcasted_iota(jnp.int32, (rows - CTX * TILE, rows_in), 1)
    place = ri % per * seq + ri // per % 2 * half_seq + ri // TILE
    main = jnp.where(ci == place, 1.0, 0.0).astype(jnp.bfloat16)
    rc = lax.broadcasted_iota(jnp.int32, (CTX * TILE, rows_in), 0)
    cc = lax.broadcasted_iota(jnp.int32, (CTX * TILE, rows_in), 1)

    for g in range(groups):
        back = jnp.concatenate([c0[g * per : (g + 1) * per]] * (CTX * 2), axis=0) - CTX + rc // TILE
        hits = (cc == rc % per * seq + back) & (back >= 0) & (rc // per % 2 == 1)
        sel[g, : CTX * TILE, :] = jnp.where(hits, 1.0, 0.0).astype(jnp.bfloat16)
        sel[g, CTX * TILE :, :] = main

    def project(w_ref, blocks):
        n = len(blocks) * cols

        def ordered(g, carry):
            h = hid[pl.ds(pl.multiple_of(g * rows_in, rows_in), rows_in), :]
            p = jnp.dot(h, w_ref[...], preferred_element_type=jnp.float32).astype(jnp.bfloat16)
            q = jnp.dot(sel[g], p, preferred_element_type=jnp.float32).astype(jnp.bfloat16)
            at = pl.ds(pl.multiple_of(g * TILE, TILE), TILE)
            framed[:, at, :n] = q.reshape(frames, TILE, n)
            return carry

        def spread(t, carry):
            v = jnp.dot(pick[...], framed[t, :, :n], preferred_element_type=jnp.float32)
            v = v.astype(jnp.bfloat16)
            at = pl.ds(pl.multiple_of(t * slots, slots), slots)
            for i, b in enumerate(blocks):
                part = v[:, i * cols : (i + 1) * cols]
                pbuf[b, :, :, at, :] = part.reshape(2, n_y, slots, cols)
            return carry

        if blocks[0] == 0:
            head_load.wait()
            for n_load in range(LOADS):
                loads[n_load].wait()
                for g in range(groups // LOADS):
                    ordered(n_load * (groups // LOADS) + g, 0)
        else:
            twice(groups, ordered, 4)
        twice(frames, spread, 7)

    project(head, (0,))
    pl.semaphore_wait(barrier, 8)

    def pair(b):
        send(pbuf.at[b, 0], sib.at[b], pair_s.at[b], pair_r.at[b], sibling)

    def own(b, k):
        return pbuf[b, 1, k].astype(jnp.float32) + sib[b, k].astype(jnp.float32)

    def step(b, s):
        if s == 0:
            arrived(sib.at[b], pair_s.at[b], pair_r.at[b])
            v = own(b, n_y // 2).astype(jnp.bfloat16)
            tx0[b, 0] = v[:mid]
            tx0[b, 1] = v[mid:]
            for d in range(2):
                send(tx0.at[b, d], rx0.at[b, d], ring_s.at[b, d, 0], ring_r.at[b, d, 0], ring[d])
            return
        for d in range(2):
            k = n_y // 2 - s if d == 0 else n_y // 2 + s
            v = own(b, k)
            if s == 1:
                arrived(rx0.at[b, d], ring_s.at[b, d, 0], ring_r.at[b, d, 0])
                more = rx0[b, d].astype(jnp.float32)
                if d == 0:
                    v = jnp.concatenate([v[:mid] + more, v[mid:]], axis=0)
                else:
                    v = jnp.concatenate([v[:mid], v[mid:] + more], axis=0)
            else:
                arrived(rx.at[b, d, s - 2], ring_s.at[b, d, s - 1], ring_r.at[b, d, s - 1])
                v = v + rx[b, d, s - 2].astype(jnp.float32)
            tx[b, d, s - 1] = v.astype(jnp.bfloat16)
            send(tx.at[b, d, s - 1], rx.at[b, d, s - 1], ring_s.at[b, d, s], ring_r.at[b, d, s], ring[d])

    def final(b):
        v = own(b, 0)
        last = n_y // 2 - 1
        for d in range(2):
            arrived(rx.at[b, d, last - 1], ring_s.at[b, d, last], ring_r.at[b, d, last])
            v = v + rx[b, d, last - 1].astype(jnp.float32)
        q = xi if b == 0 else origin[b - 1]
        x[:, pl.ds(pl.multiple_of(q * cols, cols), cols)] = v.astype(jnp.bfloat16)

    def head_ref(j):
        return hw1 if j == 2 else hw2.at[:, pl.ds(j * cols, cols)]

    def head_send(j):
        send(head, head_ref(j), head_s.at[j], head_r.at[j], across[j])

    def head_in(*js):
        for j in js:
            arrived(head_ref(j), head_s.at[j], head_r.at[j])
        project(hw1 if js == (2,) else hw2, tuple(j + 1 for j in js))
        for j in js:
            pair(j + 1)

    half, quarter = piece // 2, piece // 4
    e = lax.rem(zi, 2)

    def up_rows(q, offset, n):
        return wup.at[:, pl.ds(pl.multiple_of(q * piece + offset, n), n), :]

    def upx_send(j):
        mine = wupin.at[:, pl.ds(pl.multiple_of(c * half + e * quarter, quarter), quarter), :]
        send(mine, up_rows(xi, c * half + e * quarter, quarter), upx_s.at[j], upx_r.at[j], across[j])

    def upx_in(j):
        at = c * half + e * quarter
        arrived(up_rows(origin[j], at, quarter), upx_s.at[j], upx_r.at[j])
        for d in range(2):
            ref = up_rows(origin[j], at + d * (quarter // 2), quarter // 2)
            send(ref, ref, upz_s.at[j, d], upz_r.at[j, d], updown[d])

    def upz_in(j):
        at = c * half + (1 - e) * quarter
        for d in range(2):
            ref = up_rows(origin[j], at + d * (quarter // 2), quarter // 2)
            arrived(ref, upz_s.at[j, d], upz_r.at[j, d])
        ref = up_rows(origin[j], c * half, half)
        send(ref, ref, upc_s.at[j], upc_r.at[j], sibling)

    def upc_in(j):
        arrived(up_rows(origin[j], (1 - c) * half, half), upc_s.at[j], upc_r.at[j])

    head_send(0)
    head_send(1)
    pair(0)
    step(0, 0)
    head_send(2)
    head_in(0, 1)
    upx_send(0)
    upx_send(1)
    step(0, 1)
    head_in(2)
    upx_send(2)
    step(1, 0)
    step(2, 0)
    step(0, 2)
    step(3, 0)
    step(1, 1)
    step(2, 1)
    step(0, 3)
    step(3, 1)
    upx_in(0)
    upx_in(1)
    step(1, 2)
    step(2, 2)
    final(0)
    step(3, 2)
    upx_in(2)
    step(1, 3)
    step(2, 3)
    upz_in(0)
    upz_in(1)
    step(3, 3)
    final(1)
    final(2)
    upz_in(2)
    final(3)
    for j in range(3):
        upc_in(j)
    for copy in others:
        copy.wait()
    for copy in sent:
        copy.wait_send()
    vocode(
        slots, frames, stride, count, second,
        x, wup, bias, a1, dw, a2, pw, out, up, act, out32,
    )


def body(
    hidden,
    latent_head_weight,
    stretch_holder,
    stretch_position,
    stretch_frame_count,
    upsample_weight,
    upsample_bias,
    snake_alpha_first,
    dilated_weight,
    snake_alpha_second,
    pointwise_weight,
):
    n_z, n_mp, n_x = lax.axis_size("pipe"), lax.axis_size("mp"), lax.axis_size("dp")
    n_y = n_mp // 2
    streams = stretch_frame_count.shape[0]
    items = 2 * streams
    seq_len = hidden.shape[0] // streams
    stretch_len = seq_len // 2
    slots = 2 * items // n_mp
    frames = stretch_len + CTX
    rows = frames * slots
    width = upsample_bias.shape[0]
    stride = upsample_weight.shape[2] // width
    span = stretch_len * stride
    depth, cols = latent_head_weight.shape
    latent = cols * n_x

    vmem = pl.BlockSpec(memory_space=pltpu.VMEM)
    anywhere = pl.BlockSpec(memory_space=pl.ANY)
    bf16, f32 = jnp.bfloat16, jnp.float32
    dma = pltpu.SemaphoreType.DMA
    out = pl.pallas_call(
        functools.partial(kernel, slots, frames, stride, n_z, n_y, n_x),
        out_shape=jax.ShapeDtypeStruct((slots, span, width), bf16),
        in_specs=[vmem] * 6 + [anywhere] * 5,
        out_specs=vmem,
        scratch_shapes=[
            pltpu.VMEM(hidden.shape, bf16),
            pltpu.VMEM((depth, cols), bf16),
            pltpu.VMEM(dilated_weight.shape, bf16),
            pltpu.VMEM(pointwise_weight.shape, bf16),
            pltpu.VMEM((items // TILE, rows, TILE // 2 * seq_len), bf16),
            pltpu.VMEM((n_mp * slots, items), bf16),
            pltpu.VMEM((frames, items, 2 * cols), bf16),
            pltpu.VMEM((depth, 2 * cols), bf16),
            pltpu.VMEM((depth, cols), bf16),
            pltpu.VMEM((BLOCKS, 2, n_y, rows, cols), bf16),
            pltpu.VMEM((BLOCKS, n_y, rows, cols), bf16),
            pltpu.VMEM((BLOCKS, 2, rows // 2, cols), bf16),
            pltpu.VMEM((BLOCKS, 2, 3, rows, cols), bf16),
            pltpu.VMEM((BLOCKS, 2, rows // 2, cols), bf16),
            pltpu.VMEM((BLOCKS, 2, 3, rows, cols), bf16),
            pltpu.VMEM((rows, latent), bf16),
            pltpu.VMEM((2, latent, stride * width), bf16),
            pltpu.VMEM((stride, rows - CTX * slots, width), f32),
            pltpu.VMEM((stride, rows - slots, width), bf16),
            pltpu.VMEM((2, slots * span, width // 2), f32),
            dma((LOADS + 4,)),
            dma((3,)), dma((3,)),
            dma((BLOCKS,)), dma((BLOCKS,)),
            dma((BLOCKS, 2, 4)), dma((BLOCKS, 2, 4)),
            dma((3,)), dma((3,)),
            dma((3, 2)), dma((3, 2)),
            dma((3,)), dma((3,)),
        ],
        compiler_params=pltpu.CompilerParams(
            collective_id=0, has_side_effects=True, vmem_limit_bytes=56 * 2**20
        ),
    )(
        stretch_holder.T, stretch_position.T, stretch_frame_count.T,
        upsample_bias[None], snake_alpha_first[None], snake_alpha_second[None],
        hidden, latent_head_weight, upsample_weight, dilated_weight, pointwise_weight,
    )
    return out.reshape(1, slots, 1, span, width)


def solution(mesh):
    in_specs = (
        P(("pipe", "dp"), "mp"),
        P("mp", "dp"),
        P(("pipe", "dp"), None),
        P(("pipe", "dp"), None),
        P(("pipe", "dp"), None),
        P(None, "dp", None),
        P(),
        P(),
        P(),
        P(),
        P(),
    )
    out_specs = P("pipe", "mp", "dp", None, None)
    return jax.shard_map(body, mesh=mesh, in_specs=in_specs, out_specs=out_specs, check_vma=False)
```

```python
import functools

import jax
import jax.numpy as jnp
from jax import lax
from jax.experimental import pallas as pl
from jax.experimental.pallas import tpu as pltpu
from jax.sharding import PartitionSpec as P

DILATION_RATE = 3
CTX = 2
TILE = 16
BLOCKS = 4
LOADS = 4
EARLY = True
MESH = pl.DeviceIdType.MESH

SIN2 = (
    9.869604110717773,
    -32.469669342041016,
    42.727195739746094,
    -30.101465225219727,
    13.05009937286377,
    -3.3565926551818848,
)


def snake(v, turns, inverse):
    u = v * turns
    r = u - jnp.round(u)
    s = r * r
    q = jnp.full_like(s, SIN2[-1])
    for c in SIN2[-2::-1]:
        q = q * s + c
    return v + (q * s) * inverse


def twice(n, step, per=2):
    if n == per:
        for j in range(n):
            step(j, 0)
        return

    def some(i, carry):
        for j in range(per):
            step(per * i + j, carry)
        return carry

    lax.fori_loop(0, n // per, some, 0)


def vocode(slots, frames, stride, count, second, x_ref, wup, bias, a1, dw, a2, pw, out_ref, up, act, out32):
    rows = frames * slots
    live = rows - CTX * slots
    width = bias.shape[1]
    half = width // 2
    span = (frames - CTX) * stride
    turns1 = a1[...] * (1.0 / jnp.pi)
    inv1 = 1.0 / a1[...]
    turns2 = a2[...] * (1.0 / jnp.pi)
    inv2 = 1.0 / a2[...]
    both = jnp.concatenate(
        [x_ref[pl.ds(slots, rows - slots), :], x_ref[pl.ds(0, rows - slots), :]], axis=1
    )

    def first(r, carry):
        col = pl.ds(r * width, width)
        w = jnp.concatenate([wup[0, :, col], wup[1, :, col]], axis=0)
        u = jnp.dot(both, w, preferred_element_type=jnp.float32) + bias[...]
        u = jnp.concatenate([jnp.where(second, u[:slots], 0.0), u[slots:]], axis=0)
        up[r] = u[slots:]
        act[r] = snake(u, turns1, inv1).astype(jnp.bfloat16)
        return carry

    twice(stride, first, stride)

    def tap(r, back):
        s = r - back
        if s >= 0:
            return act[s, pl.ds(slots, live), :]
        return act[s + stride, pl.ds(0, live), :]

    def second_half(r, carry):
        taps = jnp.concatenate([tap(r, j * DILATION_RATE) for j in range(3)], axis=1)
        d = jnp.dot(taps, dw[...].reshape(3 * width, width), preferred_element_type=jnp.float32)
        b = snake(d, turns2, inv2).astype(jnp.bfloat16)
        o = up[r] + jnp.dot(b, pw[...], preferred_element_type=jnp.float32)
        for t in range(frames - CTX):
            piece = jnp.where(count > t, o[t * slots : (t + 1) * slots], 0.0)
            at = pl.ds(t * stride + r, slots, stride=span)
            out32[0, at, :] = piece[:, :half]
            out32[1, at, :] = piece[:, half:]
        return carry

    twice(stride, second_half, stride)

    def pack(s, carry):
        at = pl.ds(pl.multiple_of(s * span, span), span)
        out_ref[s] = jnp.concatenate([out32[0, at, :], out32[1, at, :]], axis=1).astype(
            out_ref.dtype
        )
        return carry

    twice(slots, pack, 4)


def kernel(
    slots, frames, stride, n_z, n_y, n_x,
    holder, position, counts, bias, a1, a2, hidden, headin, wupin, dwin, pwin,
    out,
    hid, head, dw, pw, sel, pick, framed, hw2, hw1, pbuf, sib, rx0, rx, tx0, tx, x, wup, up, act, out32,
    local_sem, head_s, head_r, pair_s, pair_r, ring_s, ring_r, upx_s, upx_r, upf_s, upf_r, upz_s, upz_r, upc_s, upc_r,
):
    zi, mi, xi = lax.axis_index("pipe"), lax.axis_index("mp"), lax.axis_index("dp")
    y, c = lax.div(mi, 2), lax.rem(mi, 2)
    rows = frames * slots
    mid = rows // 2
    cols = headin.shape[1]

    def peer(dz=0, dy=0, dc=0, dx=0):
        return (
            lax.rem(zi + dz + n_z, n_z),
            lax.rem(y + dy + n_y, n_y) * 2 + lax.rem(c + dc, 2),
            lax.rem(xi + dx + n_x, n_x),
        )

    sibling = peer(dc=1)
    ring = (peer(dy=1), peer(dy=-1))
    across = (peer(dx=1), peer(dx=-1), peer(dx=2))
    origin = (lax.rem(xi + n_x - 1, n_x), lax.rem(xi + 1, n_x), lax.rem(xi + 2, n_x))
    updown = (peer(dz=1), peer(dz=-1))
    sent = []

    def remote(src_ref, dst_ref, s, r, to):
        return pltpu.make_async_remote_copy(
            src_ref=src_ref, dst_ref=dst_ref, send_sem=s, recv_sem=r, device_id=to, device_id_type=MESH
        )

    def send(*a):
        copy = remote(*a)
        copy.start()
        sent.append(copy)

    def arrived(ref, s, r):
        remote(ref, ref, s, r, sibling).wait_recv()

    streams = holder.shape[1]
    items = 2 * streams
    per = TILE // 2
    groups = streams // per
    seq = hid.shape[0] // streams
    half_seq = seq // 2
    rows_in = per * seq
    chunk = hid.shape[0] // LOADS
    loads = [
        pltpu.make_async_copy(
            hidden.at[pl.ds(n * chunk, chunk)], hid.at[pl.ds(n * chunk, chunk)], local_sem.at[n]
        )
        for n in range(LOADS)
    ]
    piece = wupin.shape[1]
    head_load = pltpu.make_async_copy(headin, head, local_sem.at[LOADS])
    others = [
        pltpu.make_async_copy(
            wupin,
            wup.at[:, pl.ds(pl.multiple_of(xi * piece, piece), piece), :],
            local_sem.at[LOADS + 1],
        ),
        pltpu.make_async_copy(dwin, dw, local_sem.at[LOADS + 2]),
        pltpu.make_async_copy(pwin, pw, local_sem.at[LOADS + 3]),
    ]
    for copy in (head_load, *loads, *others):
        copy.start()
    barrier = pltpu.get_barrier_semaphore()
    for other in (sibling, *ring, *across, *updown):
        pl.semaphore_signal(barrier, inc=1, device_id=other, device_id_type=MESH)

    s_of = lax.broadcasted_iota(jnp.int32, (streams, items), 0)
    lane = lax.broadcasted_iota(jnp.int32, (streams, items), 1)
    mine = s_of == lane // TILE * per + lane % per
    late = lane // per % 2 == 1

    eye = lax.broadcasted_iota(jnp.int32, (streams, streams), 0) == lax.broadcasted_iota(
        jnp.int32, (streams, streams), 1
    )

    def column(v):
        return jnp.sum(jnp.where(eye, v, 0), axis=1, keepdims=True)

    def along(first, later):
        v = jnp.where(mine, jnp.where(late, later, first), 0)
        return jnp.sum(v, axis=0, keepdims=True)

    key = holder[...] * slots + position[...]
    length = counts[...]
    c0 = column(length[0:1])
    keys = along(column(key[0:1]), column(key[1:2]))
    lengths = along(c0, column(length[1:2]))

    r = lax.broadcasted_iota(jnp.int32, (n_y * 2 * slots, items), 0)
    core = (r // (n_y * slots) + c + 1) % 2
    owner = (r // slots % n_y + y) % n_y * 2 + core
    pick[...] = jnp.where(keys == owner * slots + r % slots, 1.0, 0.0).astype(jnp.bfloat16)

    own_slot = lax.broadcasted_iota(jnp.int32, (slots, items), 0) + mi * slots
    hit = keys == own_slot
    count = jnp.sum(jnp.where(hit, lengths, 0), axis=1, keepdims=True)
    is_late = lax.broadcasted_iota(jnp.int32, (slots, items), 1) // per % 2
    second = jnp.sum(jnp.where(hit, is_late, 0), axis=1, keepdims=True) > 0

    ri = lax.broadcasted_iota(jnp.int32, (rows - CTX * TILE, rows_in), 0)
    ci = lax.broadcasted_iota(jnp.int32, (rows - CTX * TILE, rows_in), 1)
    place = ri % per * seq + ri // per % 2 * half_seq + ri // TILE
    main = jnp.where(ci == place, 1.0, 0.0).astype(jnp.bfloat16)
    rc = lax.broadcasted_iota(jnp.int32, (CTX * TILE, rows_in), 0)
    cc = lax.broadcasted_iota(jnp.int32, (CTX * TILE, rows_in), 1)

    for g in range(groups):
        back = jnp.concatenate([c0[g * per : (g + 1) * per]] * (CTX * 2), axis=0) - CTX + rc // TILE
        hits = (cc == rc % per * seq + back) & (back >= 0) & (rc // per % 2 == 1)
        sel[g, : CTX * TILE, :] = jnp.where(hits, 1.0, 0.0).astype(jnp.bfloat16)
        sel[g, CTX * TILE :, :] = main

    def project(w_ref, blocks):
        n = len(blocks) * cols

        def ordered(g, carry):
            h = hid[pl.ds(g * rows_in, rows_in), :]
            p = jnp.dot(h, w_ref[...], preferred_element_type=jnp.float32).astype(jnp.bfloat16)
            q = jnp.dot(sel[g], p, preferred_element_type=jnp.float32).astype(jnp.bfloat16)
            at = pl.ds(g * TILE, TILE)
            framed[:, at, :n] = q.reshape(frames, TILE, n)
            return carry

        def spread(t, carry):
            v = jnp.dot(pick[...], framed[t, :, :n], preferred_element_type=jnp.float32)
            v = v.astype(jnp.bfloat16)
            at = pl.ds(t * slots, slots)
            for i, b in enumerate(blocks):
                part = v[:, i * cols : (i + 1) * cols]
                pbuf[b, :, :, at, :] = part.reshape(2, n_y, slots, cols)
            return carry

        if blocks[0] == 0:
            head_load.wait()
            for n_load in range(LOADS):
                loads[n_load].wait()
                for g in range(groups // LOADS):
                    ordered(n_load * (groups // LOADS) + g, 0)
        else:
            twice(groups, ordered, groups)
        twice(frames, spread, frames)

    project(head, (0,))
    pl.semaphore_wait(barrier, 8)

    def pair(b):
        send(pbuf.at[b, 0], sib.at[b], pair_s.at[b], pair_r.at[b], sibling)

    def own(b, k):
        return pbuf[b, 1, k].astype(jnp.float32) + sib[b, k].astype(jnp.float32)

    def step(b, s):
        if s == 0:
            arrived(sib.at[b], pair_s.at[b], pair_r.at[b])
            v = own(b, n_y // 2).astype(jnp.bfloat16)
            tx0[b, 0] = v[:mid]
            tx0[b, 1] = v[mid:]
            for d in range(2):
                send(tx0.at[b, d], rx0.at[b, d], ring_s.at[b, d, 0], ring_r.at[b, d, 0], ring[d])
            return
        for d in range(2):
            k = n_y // 2 - s if d == 0 else n_y // 2 + s
            v = own(b, k)
            if s == 1:
                arrived(rx0.at[b, d], ring_s.at[b, d, 0], ring_r.at[b, d, 0])
                more = rx0[b, d].astype(jnp.float32)
                if d == 0:
                    v = jnp.concatenate([v[:mid] + more, v[mid:]], axis=0)
                else:
                    v = jnp.concatenate([v[:mid], v[mid:] + more], axis=0)
            else:
                arrived(rx.at[b, d, s - 2], ring_s.at[b, d, s - 1], ring_r.at[b, d, s - 1])
                v = v + rx[b, d, s - 2].astype(jnp.float32)
            tx[b, d, s - 1] = v.astype(jnp.bfloat16)
            send(tx.at[b, d, s - 1], rx.at[b, d, s - 1], ring_s.at[b, d, s], ring_r.at[b, d, s], ring[d])

    def final(b):
        v = own(b, 0)
        last = n_y // 2 - 1
        for d in range(2):
            arrived(rx.at[b, d, last - 1], ring_s.at[b, d, last], ring_r.at[b, d, last])
            v = v + rx[b, d, last - 1].astype(jnp.float32)
        q = xi if b == 0 else origin[b - 1]
        x[:, pl.ds(pl.multiple_of(q * cols, cols), cols)] = v.astype(jnp.bfloat16)

    def head_ref(j):
        return hw1 if j == 2 else hw2.at[:, pl.ds(j * cols, cols)]

    def head_send(j):
        send(head, head_ref(j), head_s.at[j], head_r.at[j], across[j])

    half, quarter = piece // 2, piece // 4
    e = lax.rem(zi, 2)

    def up_rows(q, offset, n):
        return wup.at[:, pl.ds(pl.multiple_of(q * piece + offset, n), n), :]

    def upx_send(j):
        mine = wupin.at[:, pl.ds(pl.multiple_of(c * half + e * quarter, quarter), quarter), :]
        send(mine, up_rows(xi, c * half + e * quarter, quarter), upx_s.at[j], upx_r.at[j], across[j])

    def head_in(*js):
        for j in js:
            arrived(head_ref(j), head_s.at[j], head_r.at[j])
        for j in js:
            if j < 2 and EARLY:
                upx_send(j)
        project(hw1 if js == (2,) else hw2, tuple(j + 1 for j in js))
        for j in js:
            pair(j + 1)

    def upx_in(j):
        at = c * half + e * quarter
        pieces = [up_rows(origin[j], at + d * (quarter // 2), quarter // 2) for d in range(2)]
        if j < 2:
            arrived(up_rows(origin[j], at, quarter), upx_s.at[j], upx_r.at[j])
            send(pieces[j], pieces[j], upf_s.at[j], upf_r.at[j], across[j])
        for d in range(2):
            if j == 2:
                arrived(pieces[d], upf_s.at[d], upf_r.at[d])
            send(pieces[d], pieces[d], upz_s.at[j, d], upz_r.at[j, d], updown[d])

    def upz_in(j):
        at = c * half + (1 - e) * quarter
        for d in range(2):
            ref = up_rows(origin[j], at + d * (quarter // 2), quarter // 2)
            arrived(ref, upz_s.at[j, d], upz_r.at[j, d])
        ref = up_rows(origin[j], c * half, half)
        send(ref, ref, upc_s.at[j], upc_r.at[j], sibling)

    def upc_in(j):
        arrived(up_rows(origin[j], (1 - c) * half, half), upc_s.at[j], upc_r.at[j])

    head_send(0)
    head_send(1)
    pair(0)
    step(0, 0)
    head_send(2)
    head_in(0, 1)
    step(0, 1)
    head_in(2)
    step(1, 0)
    step(2, 0)
    step(0, 2)
    step(3, 0)
    step(1, 1)
    step(2, 1)
    step(0, 3)
    step(3, 1)
    upx_in(0)
    upx_in(1)
    step(1, 2)
    step(2, 2)
    final(0)
    step(3, 2)
    upx_in(2)
    step(1, 3)
    step(2, 3)
    upz_in(0)
    upz_in(1)
    step(3, 3)
    final(1)
    final(2)
    upz_in(2)
    final(3)
    for j in range(3):
        upc_in(j)
    for copy in others:
        copy.wait()
    vocode(
        slots, frames, stride, count, second,
        x, wup, bias, a1, dw, a2, pw, out, up, act, out32,
    )
    for copy in sent:
        copy.wait_send()


def body(
    hidden,
    latent_head_weight,
    stretch_holder,
    stretch_position,
    stretch_frame_count,
    upsample_weight,
    upsample_bias,
    snake_alpha_first,
    dilated_weight,
    snake_alpha_second,
    pointwise_weight,
):
    n_z, n_mp, n_x = lax.axis_size("pipe"), lax.axis_size("mp"), lax.axis_size("dp")
    n_y = n_mp // 2
    streams = stretch_frame_count.shape[0]
    items = 2 * streams
    seq_len = hidden.shape[0] // streams
    stretch_len = seq_len // 2
    slots = 2 * items // n_mp
    frames = stretch_len + CTX
    rows = frames * slots
    width = upsample_bias.shape[0]
    stride = upsample_weight.shape[2] // width
    span = stretch_len * stride
    depth, cols = latent_head_weight.shape
    latent = cols * n_x

    vmem = pl.BlockSpec(memory_space=pltpu.VMEM)
    anywhere = pl.BlockSpec(memory_space=pl.ANY)
    bf16, f32 = jnp.bfloat16, jnp.float32
    dma = pltpu.SemaphoreType.DMA
    out = pl.pallas_call(
        functools.partial(kernel, slots, frames, stride, n_z, n_y, n_x),
        out_shape=jax.ShapeDtypeStruct((slots, span, width), bf16),
        in_specs=[vmem] * 6 + [anywhere] * 5,
        out_specs=vmem,
        scratch_shapes=[
            pltpu.VMEM(hidden.shape, bf16),
            pltpu.VMEM((depth, cols), bf16),
            pltpu.VMEM(dilated_weight.shape, bf16),
            pltpu.VMEM(pointwise_weight.shape, bf16),
            pltpu.VMEM((items // TILE, rows, TILE // 2 * seq_len), bf16),
            pltpu.VMEM((n_mp * slots, items), bf16),
            pltpu.VMEM((frames, items, 2 * cols), bf16),
            pltpu.VMEM((depth, 2 * cols), bf16),
            pltpu.VMEM((depth, cols), bf16),
            pltpu.VMEM((BLOCKS, 2, n_y, rows, cols), bf16),
            pltpu.VMEM((BLOCKS, n_y, rows, cols), bf16),
            pltpu.VMEM((BLOCKS, 2, rows // 2, cols), bf16),
            pltpu.VMEM((BLOCKS, 2, 3, rows, cols), bf16),
            pltpu.VMEM((BLOCKS, 2, rows // 2, cols), bf16),
            pltpu.VMEM((BLOCKS, 2, 3, rows, cols), bf16),
            pltpu.VMEM((rows, latent), bf16),
            pltpu.VMEM((2, latent, stride * width), bf16),
            pltpu.VMEM((stride, rows - CTX * slots, width), f32),
            pltpu.VMEM((stride, rows - slots, width), bf16),
            pltpu.VMEM((2, slots * span, width // 2), f32),
            dma((LOADS + 4,)),
            dma((3,)), dma((3,)),
            dma((BLOCKS,)), dma((BLOCKS,)),
            dma((BLOCKS, 2, 4)), dma((BLOCKS, 2, 4)),
            dma((2,)), dma((2,)),
            dma((2,)), dma((2,)),
            dma((3, 2)), dma((3, 2)),
            dma((3,)), dma((3,)),
        ],
        compiler_params=pltpu.CompilerParams(
            collective_id=0, has_side_effects=True, vmem_limit_bytes=56 * 2**20
        ),
    )(
        stretch_holder.T, stretch_position.T, stretch_frame_count.T,
        upsample_bias[None], snake_alpha_first[None], snake_alpha_second[None],
        hidden, latent_head_weight, upsample_weight, dilated_weight, pointwise_weight,
    )
    return out.reshape(1, slots, 1, span, width)


def solution(mesh):
    in_specs = (
        P(("pipe", "dp"), "mp"),
        P("mp", "dp"),
        P(("pipe", "dp"), None),
        P(("pipe", "dp"), None),
        P(("pipe", "dp"), None),
        P(None, "dp", None),
        P(),
        P(),
        P(),
        P(),
        P(),
    )
    out_specs = P("pipe", "mp", "dp", None, None)
    return jax.shard_map(body, mesh=mesh, in_specs=in_specs, out_specs=out_specs, check_vma=False)
```

```python
import functools

import jax
import jax.numpy as jnp
from jax import lax
from jax.experimental import pallas as pl
from jax.experimental.pallas import tpu as pltpu
from jax.sharding import PartitionSpec as P

DILATION_RATE = 3
CTX = 2
TILE = 16
BLOCKS = 4
LOADS = 4
EARLY = True
MESH = pl.DeviceIdType.MESH

SIN2 = (
    9.869604110717773,
    -32.469669342041016,
    42.727195739746094,
    -30.101465225219727,
    13.05009937286377,
    -3.3565926551818848,
)


def snake(v, turns, inverse):
    u = v * turns
    r = u - jnp.round(u)
    s = r * r
    q = jnp.full_like(s, SIN2[-1])
    for c in SIN2[-2::-1]:
        q = q * s + c
    return v + (q * s) * inverse


def twice(n, step, per=2):
    if n == per:
        for j in range(n):
            step(j, 0)
        return

    def some(i, carry):
        for j in range(per):
            step(per * i + j, carry)
        return carry

    lax.fori_loop(0, n // per, some, 0)


def vocode(slots, frames, stride, count, second, x_ref, wup, bias, a1, dw, a2, pw, out_ref, up, act, out32):
    rows = frames * slots
    live = rows - CTX * slots
    width = bias.shape[1]
    half = width // 2
    span = (frames - CTX) * stride
    turns1 = a1[...] * (1.0 / jnp.pi)
    inv1 = 1.0 / a1[...]
    turns2 = a2[...] * (1.0 / jnp.pi)
    inv2 = 1.0 / a2[...]
    both = jnp.concatenate(
        [x_ref[pl.ds(slots, rows - slots), :], x_ref[pl.ds(0, rows - slots), :]], axis=1
    )

    def first(r, carry):
        col = pl.ds(r * width, width)
        w = jnp.concatenate([wup[0, :, col], wup[1, :, col]], axis=0)
        u = jnp.dot(both, w, preferred_element_type=jnp.float32) + bias[...]
        u = jnp.concatenate([jnp.where(second, u[:slots], 0.0), u[slots:]], axis=0)
        up[r] = u[slots:]
        act[r] = snake(u, turns1, inv1).astype(jnp.bfloat16)
        return carry

    twice(stride, first, stride)

    def tap(r, back):
        s = r - back
        if s >= 0:
            return act[s, pl.ds(slots, live), :]
        return act[s + stride, pl.ds(0, live), :]

    def second_half(r, carry):
        taps = jnp.concatenate([tap(r, j * DILATION_RATE) for j in range(3)], axis=1)
        d = jnp.dot(taps, dw[...].reshape(3 * width, width), preferred_element_type=jnp.float32)
        b = snake(d, turns2, inv2).astype(jnp.bfloat16)
        o = up[r] + jnp.dot(b, pw[...], preferred_element_type=jnp.float32)
        for t in range(frames - CTX):
            piece = jnp.where(count > t, o[t * slots : (t + 1) * slots], 0.0)
            at = pl.ds(t * stride + r, slots, stride=span)
            out32[0, at, :] = piece[:, :half]
            out32[1, at, :] = piece[:, half:]
        return carry

    twice(stride, second_half, stride)

    def pack(s, carry):
        at = pl.ds(s * span, span)
        out_ref[s] = jnp.concatenate([out32[0, at, :], out32[1, at, :]], axis=1).astype(
            out_ref.dtype
        )
        return carry

    twice(slots, pack, slots)


def kernel(
    slots, frames, stride, n_z, n_y, n_x,
    holder, position, counts, bias, a1, a2, hidden, headin, wupin, dwin, pwin,
    out,
    hid, head, dw, pw, sel, pick, framed, hw2, hw1, pbuf, sib, rx0, rx, tx0, tx, x, wup, up, act, out32,
    local_sem, head_s, head_r, pair_s, pair_r, ring_s, ring_r, upx_s, upx_r, upf_s, upf_r, upz_s, upz_r, upc_s, upc_r,
):
    zi, mi, xi = lax.axis_index("pipe"), lax.axis_index("mp"), lax.axis_index("dp")
    y, c = lax.div(mi, 2), lax.rem(mi, 2)
    rows = frames * slots
    mid = rows // 2
    cols = headin.shape[1]

    def peer(dz=0, dy=0, dc=0, dx=0):
        return (
            lax.rem(zi + dz + n_z, n_z),
            lax.rem(y + dy + n_y, n_y) * 2 + lax.rem(c + dc, 2),
            lax.rem(xi + dx + n_x, n_x),
        )

    sibling = peer(dc=1)
    ring = (peer(dy=1), peer(dy=-1))
    across = (peer(dx=1), peer(dx=-1), peer(dx=2))
    origin = (lax.rem(xi + n_x - 1, n_x), lax.rem(xi + 1, n_x), lax.rem(xi + 2, n_x))
    updown = (peer(dz=1), peer(dz=-1))
    sent = []

    def remote(src_ref, dst_ref, s, r, to):
        return pltpu.make_async_remote_copy(
            src_ref=src_ref, dst_ref=dst_ref, send_sem=s, recv_sem=r, device_id=to, device_id_type=MESH
        )

    def send(*a):
        copy = remote(*a)
        copy.start()
        sent.append(copy)

    def arrived(ref, s, r):
        remote(ref, ref, s, r, sibling).wait_recv()

    streams = holder.shape[1]
    items = 2 * streams
    per = TILE // 2
    groups = streams // per
    seq = hid.shape[0] // streams
    half_seq = seq // 2
    rows_in = per * seq
    chunk = hid.shape[0] // LOADS
    loads = [
        pltpu.make_async_copy(
            hidden.at[pl.ds(n * chunk, chunk)], hid.at[pl.ds(n * chunk, chunk)], local_sem.at[n]
        )
        for n in range(LOADS)
    ]
    piece = wupin.shape[1]
    head_load = pltpu.make_async_copy(headin, head, local_sem.at[LOADS])
    others = [
        pltpu.make_async_copy(
            wupin,
            wup.at[:, pl.ds(pl.multiple_of(xi * piece, piece), piece), :],
            local_sem.at[LOADS + 1],
        ),
        pltpu.make_async_copy(dwin, dw, local_sem.at[LOADS + 2]),
        pltpu.make_async_copy(pwin, pw, local_sem.at[LOADS + 3]),
    ]
    for copy in (head_load, *loads, *others):
        copy.start()
    barrier = pltpu.get_barrier_semaphore()
    for other in (sibling, *ring, *across, *updown):
        pl.semaphore_signal(barrier, inc=1, device_id=other, device_id_type=MESH)

    s_of = lax.broadcasted_iota(jnp.int32, (streams, items), 0)
    lane = lax.broadcasted_iota(jnp.int32, (streams, items), 1)
    mine = s_of == lane // TILE * per + lane % per
    late = lane // per % 2 == 1

    eye = lax.broadcasted_iota(jnp.int32, (streams, streams), 0) == lax.broadcasted_iota(
        jnp.int32, (streams, streams), 1
    )

    def column(v):
        return jnp.sum(jnp.where(eye, v, 0), axis=1, keepdims=True)

    def along(first, later):
        v = jnp.where(mine, jnp.where(late, later, first), 0)
        return jnp.sum(v, axis=0, keepdims=True)

    key = holder[...] * slots + position[...]
    length = counts[...]
    c0 = column(length[0:1])
    keys = along(column(key[0:1]), column(key[1:2]))
    lengths = along(c0, column(length[1:2]))

    r = lax.broadcasted_iota(jnp.int32, (n_y * 2 * slots, items), 0)
    core = (r // (n_y * slots) + c + 1) % 2
    owner = (r // slots % n_y + y) % n_y * 2 + core
    pick[...] = jnp.where(keys == owner * slots + r % slots, 1.0, 0.0).astype(jnp.bfloat16)

    own_slot = lax.broadcasted_iota(jnp.int32, (slots, items), 0) + mi * slots
    hit = keys == own_slot
    count = jnp.sum(jnp.where(hit, lengths, 0), axis=1, keepdims=True)
    is_late = lax.broadcasted_iota(jnp.int32, (slots, items), 1) // per % 2
    second = jnp.sum(jnp.where(hit, is_late, 0), axis=1, keepdims=True) > 0

    ri = lax.broadcasted_iota(jnp.int32, (rows - CTX * TILE, rows_in), 0)
    ci = lax.broadcasted_iota(jnp.int32, (rows - CTX * TILE, rows_in), 1)
    place = ri % per * seq + ri // per % 2 * half_seq + ri // TILE
    main = jnp.where(ci == place, 1.0, 0.0).astype(jnp.bfloat16)
    rc = lax.broadcasted_iota(jnp.int32, (CTX * TILE, rows_in), 0)
    cc = lax.broadcasted_iota(jnp.int32, (CTX * TILE, rows_in), 1)

    for g in range(groups):
        back = jnp.concatenate([c0[g * per : (g + 1) * per]] * (CTX * 2), axis=0) - CTX + rc // TILE
        hits = (cc == rc % per * seq + back) & (back >= 0) & (rc // per % 2 == 1)
        sel[g, : CTX * TILE, :] = jnp.where(hits, 1.0, 0.0).astype(jnp.bfloat16)
        sel[g, CTX * TILE :, :] = main

    def project(w_ref, blocks):
        n = len(blocks) * cols

        def ordered(g, carry):
            h = hid[pl.ds(g * rows_in, rows_in), :]
            p = jnp.dot(h, w_ref[...], preferred_element_type=jnp.float32).astype(jnp.bfloat16)
            q = jnp.dot(sel[g], p, preferred_element_type=jnp.float32).astype(jnp.bfloat16)
            at = pl.ds(g * TILE, TILE)
            framed[:, at, :n] = q.reshape(frames, TILE, n)
            return carry

        def spread(t, carry):
            v = jnp.dot(pick[...], framed[t, :, :n], preferred_element_type=jnp.float32)
            v = v.astype(jnp.bfloat16)
            at = pl.ds(t * slots, slots)
            for i, b in enumerate(blocks):
                part = v[:, i * cols : (i + 1) * cols]
                pbuf[b, :, :, at, :] = part.reshape(2, n_y, slots, cols)
            return carry

        if blocks[0] == 0:
            head_load.wait()
            for n_load in range(LOADS):
                loads[n_load].wait()
                for g in range(groups // LOADS):
                    ordered(n_load * (groups // LOADS) + g, 0)
        else:
            twice(groups, ordered, groups)
        twice(frames, spread, frames)

    project(head, (0,))
    pl.semaphore_wait(barrier, 8)

    def pair(b):
        send(pbuf.at[b, 0], sib.at[b], pair_s.at[b], pair_r.at[b], sibling)

    def own(b, k):
        return pbuf[b, 1, k].astype(jnp.float32) + sib[b, k].astype(jnp.float32)

    def step(b, s):
        if s == 0:
            arrived(sib.at[b], pair_s.at[b], pair_r.at[b])
            v = own(b, n_y // 2).astype(jnp.bfloat16)
            tx0[b, 0] = v[:mid]
            tx0[b, 1] = v[mid:]
            for d in range(2):
                send(tx0.at[b, d], rx0.at[b, d], ring_s.at[b, d, 0], ring_r.at[b, d, 0], ring[d])
            return
        for d in range(2):
            k = n_y // 2 - s if d == 0 else n_y // 2 + s
            v = own(b, k)
            if s == 1:
                arrived(rx0.at[b, d], ring_s.at[b, d, 0], ring_r.at[b, d, 0])
                more = rx0[b, d].astype(jnp.float32)
                if d == 0:
                    v = jnp.concatenate([v[:mid] + more, v[mid:]], axis=0)
                else:
                    v = jnp.concatenate([v[:mid], v[mid:] + more], axis=0)
            else:
                arrived(rx.at[b, d, s - 2], ring_s.at[b, d, s - 1], ring_r.at[b, d, s - 1])
                v = v + rx[b, d, s - 2].astype(jnp.float32)
            tx[b, d, s - 1] = v.astype(jnp.bfloat16)
            send(tx.at[b, d, s - 1], rx.at[b, d, s - 1], ring_s.at[b, d, s], ring_r.at[b, d, s], ring[d])

    def final(b):
        v = own(b, 0)
        last = n_y // 2 - 1
        for d in range(2):
            arrived(rx.at[b, d, last - 1], ring_s.at[b, d, last], ring_r.at[b, d, last])
            v = v + rx[b, d, last - 1].astype(jnp.float32)
        q = xi if b == 0 else origin[b - 1]
        x[:, pl.ds(pl.multiple_of(q * cols, cols), cols)] = v.astype(jnp.bfloat16)

    def head_ref(j):
        return hw1 if j == 2 else hw2.at[:, pl.ds(j * cols, cols)]

    def head_send(j):
        send(head, head_ref(j), head_s.at[j], head_r.at[j], across[j])

    half, quarter = piece // 2, piece // 4
    e = lax.rem(zi, 2)

    def up_rows(q, offset, n):
        return wup.at[:, pl.ds(pl.multiple_of(q * piece + offset, n), n), :]

    def upx_send(j):
        mine = wupin.at[:, pl.ds(pl.multiple_of(c * half + e * quarter, quarter), quarter), :]
        send(mine, up_rows(xi, c * half + e * quarter, quarter), upx_s.at[j], upx_r.at[j], across[j])

    def head_in(*js):
        for j in js:
            arrived(head_ref(j), head_s.at[j], head_r.at[j])
        for j in js:
            if j < 2 and EARLY:
                upx_send(j)
        project(hw1 if js == (2,) else hw2, tuple(j + 1 for j in js))
        for j in js:
            pair(j + 1)

    def upx_in(j):
        at = c * half + e * quarter
        pieces = [up_rows(origin[j], at + d * (quarter // 2), quarter // 2) for d in range(2)]
        if j < 2:
            arrived(up_rows(origin[j], at, quarter), upx_s.at[j], upx_r.at[j])
            send(pieces[j], pieces[j], upf_s.at[j], upf_r.at[j], across[j])
        for d in range(2):
            if j == 2:
                arrived(pieces[d], upf_s.at[d], upf_r.at[d])
            send(pieces[d], pieces[d], upz_s.at[j, d], upz_r.at[j, d], updown[d])

    def upz_in(j):
        at = c * half + (1 - e) * quarter
        for d in range(2):
            ref = up_rows(origin[j], at + d * (quarter // 2), quarter // 2)
            arrived(ref, upz_s.at[j, d], upz_r.at[j, d])
        ref = up_rows(origin[j], c * half, half)
        send(ref, ref, upc_s.at[j], upc_r.at[j], sibling)

    def upc_in(j):
        arrived(up_rows(origin[j], (1 - c) * half, half), upc_s.at[j], upc_r.at[j])

    head_send(0)
    head_send(1)
    pair(0)
    step(0, 0)
    head_send(2)
    head_in(0, 1)
    step(0, 1)
    head_in(2)
    step(1, 0)
    step(2, 0)
    step(0, 2)
    step(3, 0)
    step(1, 1)
    step(2, 1)
    step(0, 3)
    step(3, 1)
    upx_in(0)
    upx_in(1)
    step(1, 2)
    step(2, 2)
    final(0)
    step(3, 2)
    upx_in(2)
    step(1, 3)
    step(2, 3)
    upz_in(0)
    upz_in(1)
    step(3, 3)
    final(1)
    final(2)
    upz_in(2)
    final(3)
    for j in range(3):
        upc_in(j)
    for copy in others:
        copy.wait()
    vocode(
        slots, frames, stride, count, second,
        x, wup, bias, a1, dw, a2, pw, out, up, act, out32,
    )
    for copy in sent:
        copy.wait_send()


def body(
    hidden,
    latent_head_weight,
    stretch_holder,
    stretch_position,
    stretch_frame_count,
    upsample_weight,
    upsample_bias,
    snake_alpha_first,
    dilated_weight,
    snake_alpha_second,
    pointwise_weight,
):
    n_z, n_mp, n_x = lax.axis_size("pipe"), lax.axis_size("mp"), lax.axis_size("dp")
    n_y = n_mp // 2
    streams = stretch_frame_count.shape[0]
    items = 2 * streams
    seq_len = hidden.shape[0] // streams
    stretch_len = seq_len // 2
    slots = 2 * items // n_mp
    frames = stretch_len + CTX
    rows = frames * slots
    width = upsample_bias.shape[0]
    stride = upsample_weight.shape[2] // width
    span = stretch_len * stride
    depth, cols = latent_head_weight.shape
    latent = cols * n_x

    vmem = pl.BlockSpec(memory_space=pltpu.VMEM)
    anywhere = pl.BlockSpec(memory_space=pl.ANY)
    bf16, f32 = jnp.bfloat16, jnp.float32
    dma = pltpu.SemaphoreType.DMA
    out = pl.pallas_call(
        functools.partial(kernel, slots, frames, stride, n_z, n_y, n_x),
        out_shape=jax.ShapeDtypeStruct((slots, span, width), bf16),
        in_specs=[vmem] * 6 + [anywhere] * 5,
        out_specs=vmem,
        scratch_shapes=[
            pltpu.VMEM(hidden.shape, bf16),
            pltpu.VMEM((depth, cols), bf16),
            pltpu.VMEM(dilated_weight.shape, bf16),
            pltpu.VMEM(pointwise_weight.shape, bf16),
            pltpu.VMEM((items // TILE, rows, TILE // 2 * seq_len), bf16),
            pltpu.VMEM((n_mp * slots, items), bf16),
            pltpu.VMEM((frames, items, 2 * cols), bf16),
            pltpu.VMEM((depth, 2 * cols), bf16),
            pltpu.VMEM((depth, cols), bf16),
            pltpu.VMEM((BLOCKS, 2, n_y, rows, cols), bf16),
            pltpu.VMEM((BLOCKS, n_y, rows, cols), bf16),
            pltpu.VMEM((BLOCKS, 2, rows // 2, cols), bf16),
            pltpu.VMEM((BLOCKS, 2, 3, rows, cols), bf16),
            pltpu.VMEM((BLOCKS, 2, rows // 2, cols), bf16),
            pltpu.VMEM((BLOCKS, 2, 3, rows, cols), bf16),
            pltpu.VMEM((rows, latent), bf16),
            pltpu.VMEM((2, latent, stride * width), bf16),
            pltpu.VMEM((stride, rows - CTX * slots, width), f32),
            pltpu.VMEM((stride, rows - slots, width), bf16),
            pltpu.VMEM((2, slots * span, width // 2), f32),
            dma((LOADS + 4,)),
            dma((3,)), dma((3,)),
            dma((BLOCKS,)), dma((BLOCKS,)),
            dma((BLOCKS, 2, 4)), dma((BLOCKS, 2, 4)),
            dma((2,)), dma((2,)),
            dma((2,)), dma((2,)),
            dma((3, 2)), dma((3, 2)),
            dma((3,)), dma((3,)),
        ],
        compiler_params=pltpu.CompilerParams(
            collective_id=0, has_side_effects=True, vmem_limit_bytes=56 * 2**20
        ),
    )(
        stretch_holder.T, stretch_position.T, stretch_frame_count.T,
        upsample_bias[None], snake_alpha_first[None], snake_alpha_second[None],
        hidden, latent_head_weight, upsample_weight, dilated_weight, pointwise_weight,
    )
    return out.reshape(1, slots, 1, span, width)


def solution(mesh):
    in_specs = (
        P(("pipe", "dp"), "mp"),
        P("mp", "dp"),
        P(("pipe", "dp"), None),
        P(("pipe", "dp"), None),
        P(("pipe", "dp"), None),
        P(None, "dp", None),
        P(),
        P(),
        P(),
        P(),
        P(),
    )
    out_specs = P("pipe", "mp", "dp", None, None)
    return jax.shard_map(body, mesh=mesh, in_specs=in_specs, out_specs=out_specs, check_vma=False)
```
